32 devices in a mesh: rep: 2 (over core), ep: 16 (over z, y, x).
Axes of the slice: x: 2, y: 2, z: 4, core: 2. Of those that a mesh axis runs over, the one named last changes fastest.
Arguments:
- tokens: bfloat16 [16384, 768], P(('rep', 'ep')), may hold values from -6 to 6
- cotangent: bfloat16 [16384, 768], P(('rep', 'ep')), may hold values from -6 to 6
- segment_ids: int32 [32, 512], P(('rep', 'ep')), may hold values from 0 to 3, never falling along the last dimension, each value on 1 to 256 neighbouring positions
- routes: int32 [16384, 1], P(('rep', 'ep')), may hold values from 0 to 15; in each aligned block of 512 rows (0 to 511, 512 to 1023, ...) at most 64 rows name the same one
- rel_buckets: int32 [1023], replicated, may hold values from 0 to 31
- qkv_weight: bfloat16 [768, 2304], P('ep'), may hold values from -0.21875 to 0.21875
- out_weight: bfloat16 [768, 768], P('ep'), may hold values from -1.25 to 1.25
- router_weight: bfloat16 [768, 16], replicated, may hold values from -0.109375 to 0.109375
- gains: float32 [2, 768], replicated, may hold values from 0.1 to 1.9
- bias_table: float32 [32, 12], replicated, may hold values from -4 to 4
- expert_in: bfloat16 [16, 768, 3072], P('ep'), may hold values from -0.21875 to 0.21875
- expert_out: bfloat16 [16, 3072, 768], P('ep'), may hold values from -0.109375 to 0.109375
Outputs:
- output: bfloat16 [16384, 768], P(('rep', 'ep'))
- grad_tokens: bfloat16 [16384, 768], P(('rep', 'ep'))
- grad_qkv_weight: bfloat16 [768, 2304], P('ep')
- grad_out_weight: bfloat16 [768, 768], P('ep')
- grad_router_weight: bfloat16 [768, 16], replicated
- grad_gains: bfloat16 [2, 768], replicated
- grad_bias_table: bfloat16 [32, 12], replicated
- grad_expert_in: bfloat16 [16, 768, 3072], P('ep')
- grad_expert_out: bfloat16 [16, 3072, 768], P('ep')
The draws below stay inside these ranges and needn't reach their ends.
Inputs may be any that keep to these rules, and one draw needn't show every extreme that they name: `routes`: the tokens of one device (aligned blocks of 512 rows) take at most 64 to any one expert; in every draw some device sends exactly 64 to some expert, and every expert gets some token. `segment_ids`: within each sequence the numbers never fall and each runs over 1 to 256 positions.
All inputs are finite; a program needn't handle non-finite values.
Results may differ from the reference program's by a relative error of at most 0.017.
Values may be sent and summed in bfloat16 or wider, within the bound.
A program may use at most 320 MiB of HBM per device.

```python
import math
import jax
import jax.numpy as jnp
import numpy as np
from jax import lax

D = 768
H = 12
HD = 64
FF = 3072
NB = 32
SEQ_LEN = 512
TOK_DEV = 512
EXPERTS = 16
CAP = 64
SEQS = 32
TOKENS = 16384
N_REP = 2
N_EP = 16


def touch_ends(array, own_key, least, top_value):
    longest = array.shape.index(max(array.shape))
    spots = []
    for shift in (0, 1):
        where = [jax.random.randint(jax.random.fold_in(own_key, axis), (), 0, length) for axis, length in enumerate(array.shape)]
        where[longest] = (where[longest] + shift) % array.shape[longest]
        spots.append(tuple(where))
    return array.at[spots[0]].set(least).at[spots[1]].set(top_value)


def level_of(own_key, shape, cuts, low, high):
    level = 1.0
    for position, blocks in cuts:
        steps = jax.random.uniform(jax.random.fold_in(jax.random.fold_in(own_key, 6), position), (blocks,), jnp.float32, low / len(cuts), high / len(cuts))
        level = level * jnp.repeat(jnp.exp(steps), shape[position] // blocks).reshape((-1,) + (1,) * (len(shape) - 1 - position))
    return level


def length_profile(amount, total, bound, slope):
    loads = [(1 << 20) // math.isqrt(grade ** slope) + 1 for grade in range(2, amount + 1)]
    surplus, given = total - bound - (amount - 1), [1] * (amount - 1)
    while surplus > 0:
        candidates = [i for i in range(amount - 1) if given[i] < bound]
        whole, remaining = sum([loads[i] for i in candidates]), surplus
        for i in candidates:
            extra = min(bound - given[i], max(1, remaining * loads[i] // whole), surplus)
            given[i] = given[i] + extra
            surplus = surplus - extra
    return np.array([bound] + given)


def ragged_sizes(own_key, amount, total, bound, skew):
    if amount == 2:
        one = jax.random.randint(own_key, (), max(1, total - bound), min(bound, total - 1) + 1)
        return jnp.stack([one, total - one])
    sizes = jnp.asarray(length_profile(amount, total, bound, skew), jnp.int32)
    twos = (amount - 1) // 2
    donor, receiver = sizes[1:1 + 2 * twos:2], sizes[2:2 + 2 * twos:2]
    margin = jnp.minimum(donor - 1, bound - receiver)
    passed = jax.random.randint(jax.random.fold_in(own_key, 1), (twos,), 0, 1 << 20) % (margin + 1)
    sizes = sizes.at[1:1 + 2 * twos:2].set(donor - passed).at[2:2 + 2 * twos:2].set(receiver + passed)
    return sizes[jax.random.permutation(jax.random.fold_in(own_key, 2), amount)]


def routed_block(stream_key, own, number, rows, number_of, top, reach, skew):
    sequence = jax.random.permutation(stream_key, number_of)
    crowded, usual = load_shares(number_of, rows * top, reach, skew, True), load_shares(number_of, rows * top, reach, skew, False)
    places = jnp.arange(number_of)

    def named(sizes, offset_by):
        used = int((sizes > 0).sum())
        fixed = max(1, used // 4)
        passed = fixed + (places - fixed + offset_by * (used - fixed)) % max(1, number_of - fixed)
        return jnp.zeros((number_of,), jnp.int32).at[sequence[jnp.where(places < fixed, places, passed)]].set(jnp.asarray(sizes, jnp.int32))

    sizes = jnp.where(number % 4 == 0, named(crowded, number // 4), named(usual, number - number // 4 - 1))
    mixed = jax.random.permutation(jax.random.fold_in(own, 3), number_of)
    source_of, taker = mixed[0:number_of // 2 * 2:2], mixed[1:number_of // 2 * 2:2]
    margin = jnp.minimum(sizes[source_of] - 1, reach - sizes[taker]) // 2
    margin = jnp.where((source_of == sequence[0]) | (taker == sequence[0]) | (sizes[taker] == 0), 0, jnp.maximum(margin, 0))
    passed = jax.random.randint(jax.random.fold_in(own, 4), (number_of // 2,), 0, 1 << 20) % (margin + 1)
    sizes = sizes.at[source_of].add(-passed).at[taker].add(passed)
    labels = jnp.searchsorted(jnp.cumsum(sizes), jnp.arange(rows * top), side="right").astype(jnp.int32)
    listing = labels.reshape(top, rows).T
    listing = listing[jax.random.permutation(jax.random.fold_in(own, 1), rows)]
    offset_by = jax.random.randint(jax.random.fold_in(own, 2), (rows, 1), 0, top)
    return jnp.take_along_axis(listing, (jnp.arange(top)[None, :] + offset_by) % top, axis=1)


def load_shares(count, total, most, slope, full):
    loads = [(1 << 20) // math.isqrt(grade ** slope) + 1 for grade in range(1, count + 1)]
    largest = most if full else min(most, max(-(-total // count), total * loads[0] // sum(loads)))
    least = 1 if total - largest >= count - 1 else 0
    given, surplus = [largest] + [least] * (count - 1), total - largest - least * (count - 1)
    while surplus > 0:
        candidates = [i for i in range(1, count) if given[i] < largest] or [i for i in range(1, count) if given[i] < most]
        mass, remaining = sum([loads[i] for i in candidates]), surplus
        for i in candidates:
            addition = min(most - given[i], max(1, remaining * loads[i] // mass), surplus)
            given[i] = given[i] + addition
            surplus = surplus - addition
    return np.array(given)


def scatter_about(stream_key, shape, scale, reach, split=(), kind=jnp.bfloat16):
    values = jax.random.normal(stream_key, shape, jnp.float32) * scale
    if len(split) > 0:
        values = level_of(stream_key, shape, split, -0.22, 0.18) * values
    return jnp.clip(values, min=-reach, max=reach).astype(kind)


def setup_inputs(seed: int = 0) -> dict:
    splits = jax.random.split(jax.random.key(seed), 13)
    tokens = scatter_about(splits[0], (TOKENS, D), 1.0, 6.0, ((0, 32),))
    cotangent = scatter_about(splits[1], (TOKENS, D), 1.0, 6.0, ((0, 32),))
    segment_ids = jax.vmap(lambda own: jnp.searchsorted(jnp.cumsum(ragged_sizes(own, 4, SEQ_LEN, SEQ_LEN // 2, 2)), jnp.arange(SEQ_LEN), side="right"))(jax.random.split(splits[2], SEQS)).reshape((SEQS, SEQ_LEN)).astype(jnp.int32)
    routes_keys = jax.random.split(jax.random.fold_in(splits[3], 1), TOKENS // TOK_DEV)
    routes_turns = jax.random.permutation(jax.random.fold_in(splits[3], 3), TOKENS // TOK_DEV)
    routes = jax.vmap(lambda own, number: routed_block(jax.random.fold_in(splits[3], 2), own, number, TOK_DEV, EXPERTS, 1, CAP, 2))(routes_keys, routes_turns).reshape((TOKENS, 1))
    rel_buckets = touch_ends(jax.random.randint(splits[4], (2 * SEQ_LEN - 1,), 0, NB), jax.random.fold_in(splits[4], 1), 0, NB - 1).astype(jnp.int32)
    qkv_weight = scatter_about(splits[5], (D, 3 * D), D ** -0.5, 0.21875, ((0, 16),))
    out_weight = scatter_about(splits[6], (D, D), (D // 32) ** -0.5, 1.25, ((0, 16),))
    router_weight = scatter_about(splits[7], (D, EXPERTS), (4 * D) ** -0.5, 0.109375)
    gains = jnp.clip(1.0 + 0.18 * jax.random.normal(splits[8], (2, D), jnp.float32), 0.1, 1.9)
    bias_table = scatter_about(splits[9], (NB, H), 1.0, 4.0, (), jnp.float32)
    expert_in = scatter_about(splits[10], (EXPERTS, D, FF), D ** -0.5, 0.21875, ((0, 16),))
    expert_out = scatter_about(splits[11], (EXPERTS, FF, D), FF ** -0.5, 0.109375, ((0, 16),))
    return {"tokens": tokens, "cotangent": cotangent, "segment_ids": segment_ids, "routes": routes, "rel_buckets": rel_buckets, "qkv_weight": qkv_weight, "out_weight": out_weight, "router_weight": router_weight, "gains": gains, "bias_table": bias_table, "expert_in": expert_in, "expert_out": expert_out}


@jax.custom_vjp
def low(v):
    return lax.optimization_barrier(v.astype(jnp.bfloat16)).astype(jnp.float32)

@jax.custom_vjp
def low_back(v):
    return v

def low_keep(v):
    return (low(v), None)

def low_pass(kept, grad):
    return (grad,)

def back_keep(v):
    return (v, None)

def back_low(kept, grad):
    return (low(grad),)
low.defvjp(low_keep, low_pass)
low_back.defvjp(back_keep, back_low)
epsilon = 1e-06
neg_big = -1e+30
highest = lax.Precision.HIGHEST

def rms_scale(matrix, gain_row):
    return matrix * lax.rsqrt(lax.optimization_barrier(jnp.mean(matrix * matrix, axis=-1, keepdims=True)) + epsilon) * gain_row

def attend_sequence(sequence_in, bias_cols):
    queries, key_rows, value_rows, segment = sequence_in
    sequence_length = queries.shape[0]
    offsets = lax.broadcasted_iota(jnp.int32, (sequence_length, sequence_length), 0) - lax.broadcasted_iota(jnp.int32, (sequence_length, sequence_length), 1) + (sequence_length - 1)
    position_bias_block = jnp.take(bias_cols, offsets, axis=1)
    scores = jnp.einsum('qhd,khd->hqk', queries, key_rows, precision=highest) * queries.shape[-1] ** (-0.5) + position_bias_block
    same_doc = segment[:, None] == segment[None, :]
    scores = low_back(jnp.where(same_doc[None], scores, neg_big))
    soft_low = low(jax.nn.softmax(scores, axis=-1))
    mixture = jnp.einsum('hqk,khd->qhd', soft_low, value_rows, precision=highest)
    return mixture.reshape(sequence_length, -1)

def expert_block(expert_rows):
    dispatched, weight_in, weight_out = expert_rows
    preact = low_back(jnp.dot(dispatched, weight_in, precision=highest))
    activated = low(jax.nn.gelu(preact, approximate=False))
    return jnp.dot(activated, weight_out, precision=highest)

def reference(tokens, cotangent, segment_ids, routes, rel_buckets, qkv_weight, out_weight, router_weight, gains, bias_table, expert_in, expert_out):
    devices = N_REP * N_EP
    chosen = routes[:, 0].astype(jnp.int32)
    route_hot = chosen[:, None] == jnp.arange(EXPERTS, dtype=jnp.int32)[None, :]
    running = jnp.cumsum(route_hot.reshape(devices, TOK_DEV, EXPERTS).astype(jnp.int32), axis=1).reshape(TOKENS, EXPERTS)
    slot_rank = lax.optimization_barrier(jnp.sum(jnp.where(route_hot, running, 0), axis=-1)) - 1
    owner = jnp.arange(TOKENS, dtype=jnp.int32) // TOK_DEV
    slot_index = (chosen * (devices * CAP) + owner * CAP + slot_rank).astype(jnp.int32)
    hot_float = route_hot.astype(jnp.float32)
    bucket_table = (rel_buckets[:, None] == jnp.arange(NB, dtype=jnp.int32)[None, :]).astype(jnp.float32)

    def forward(source, qkv_full, out_full, router_full, gain_pair, table, weight_in, weight_out):
        normed = low(rms_scale(source, gain_pair[0]))
        packed = low_back(low(jnp.dot(normed, qkv_full, precision=highest)))
        split_qkv = packed.reshape(SEQS, SEQ_LEN, 3, H, HD)
        bias_cols = jnp.dot(bucket_table, table, precision=highest).T
        mixture = lax.map(jax.checkpoint(lambda sequence_in: attend_sequence(sequence_in, bias_cols)), (split_qkv[:, :, 0], split_qkv[:, :, 1], split_qkv[:, :, 2], segment_ids))
        mixture = low(low_back(mixture.reshape(TOKENS, D)))
        attn_out = low_back(jnp.dot(mixture, out_full, precision=highest))
        middle = source + attn_out
        moe_in = low(rms_scale(middle, gain_pair[1]))
        logits = low_back(jnp.dot(moe_in, router_full, precision=highest))
        router = jax.nn.softmax(logits, axis=-1)
        chosen_gate_value = EXPERTS * lax.optimization_barrier(jnp.sum(router * hot_float, axis=-1))
        buffer = jnp.zeros((EXPERTS * devices * CAP, D), jnp.float32).at[slot_index].set(moe_in)
        buffer = low_back(buffer).reshape(EXPERTS, devices * CAP, D)
        produced = lax.map(jax.checkpoint(expert_block), (buffer, weight_in, weight_out))
        produced = low_back(low(produced.reshape(EXPERTS * devices * CAP, D)))
        return middle + chosen_gate_value[:, None] * produced[slot_index]
    inputs = (tokens.astype(jnp.float32), qkv_weight.astype(jnp.float32), out_weight.astype(jnp.float32), router_weight.astype(jnp.float32), gains.astype(jnp.float32), bias_table.astype(jnp.float32), expert_in.astype(jnp.float32), expert_out.astype(jnp.float32))
    result, pullback = jax.vjp(forward, *inputs)
    grads = pullback(cotangent.astype(jnp.float32))
    return (result.astype(jnp.bfloat16), grads[0].astype(jnp.bfloat16), grads[1].astype(jnp.bfloat16), grads[2].astype(jnp.bfloat16), grads[3].astype(jnp.bfloat16), grads[4].astype(jnp.bfloat16), grads[5].astype(jnp.bfloat16), grads[6].astype(jnp.bfloat16), grads[7].astype(jnp.bfloat16))
```

```python
import math

import jax
import jax.numpy as jnp
from jax import lax
from jax.experimental import pallas as pl
from jax.experimental.pallas import tpu as pltpu
from jax.sharding import PartitionSpec as P

epsilon = 1e-06
neg_big = -1e30
highest = lax.Precision.HIGHEST


def rms_scale(matrix, gain_row):
    return (
        matrix * lax.rsqrt(jnp.mean(matrix * matrix, axis=-1, keepdims=True) + epsilon) * gain_row
    )


def diagonal_bias_kernel(cols_ref, bias_ref):
    length = bias_ref.shape[1]
    rows = jnp.broadcast_to(cols_ref[0], (8, 2 * length))
    place = lax.broadcasted_iota(jnp.int32, rows.shape, 0)
    for step in (1, 2, 4):
        rows = jnp.where((place & step) != 0, pltpu.roll(rows, step, 1), rows)
    while rows.shape[0] < length:
        rows = jnp.concatenate([rows, pltpu.roll(rows, rows.shape[0], 1)], axis=0)
    bias_ref[0] = rows[:, :length]


def diagonal_bias(cols, length):
    heads = cols.shape[0]
    return pl.pallas_call(
        diagonal_bias_kernel,
        grid=(heads,),
        in_specs=[pl.BlockSpec((1, 1, 2 * length), lambda h: (h, 0, 0))],
        out_specs=pl.BlockSpec((1, length, length), lambda h: (h, 0, 0)),
        out_shape=jax.ShapeDtypeStruct((heads, length, length), jnp.float32),
        compiler_params=pltpu.CompilerParams(vmem_limit_bytes=32 * 1024 * 1024),
        cost_estimate=pl.CostEstimate(
            flops=heads * length * length * 4,
            bytes_accessed=heads * length * length * 4,
            transcendentals=0,
        ),
    )(cols[:, None, :])


def diagonal_sums_kernel(grad_ref, sums_ref):
    length = grad_ref.shape[1]
    rows = grad_ref[0].astype(jnp.float32)
    rows = jnp.concatenate([rows, jnp.zeros_like(rows)], axis=1)
    while rows.shape[0] > 8:
        half = rows.shape[0] // 2
        rows = rows[:half] + pltpu.roll(rows[half:], 2 * length - half, 1)
    place = lax.broadcasted_iota(jnp.int32, rows.shape, 0)
    for step in (4, 2, 1):
        rows = jnp.where((place & step) != 0, pltpu.roll(rows, 2 * length - step, 1), rows)
    sums_ref[0] = jnp.sum(rows, axis=0, keepdims=True)


def diagonal_sums(grad):
    heads, length, _ = grad.shape
    return pl.pallas_call(
        diagonal_sums_kernel,
        grid=(heads,),
        in_specs=[pl.BlockSpec((1, length, length), lambda h: (h, 0, 0))],
        out_specs=pl.BlockSpec((1, 1, 2 * length), lambda h: (h, 0, 0)),
        out_shape=jax.ShapeDtypeStruct((heads, 1, 2 * length), jnp.float32),
        compiler_params=pltpu.CompilerParams(vmem_limit_bytes=32 * 1024 * 1024),
        cost_estimate=pl.CostEstimate(
            flops=heads * length * length * 4,
            bytes_accessed=heads * length * length * 2,
            transcendentals=0,
        ),
    )(grad)[:, 0]


def scores_of(queries, key_rows, position_bias, segment):
    scores = (
        jnp.einsum("qhd,khd->hqk", queries, key_rows, preferred_element_type=jnp.float32)
        * queries.shape[-1] ** (-0.5)
        + position_bias
    )
    same_doc = segment[:, None] == segment[None, :]
    return jnp.where(same_doc[None], scores, neg_big)


def attend_forward(queries, key_rows, value_rows, segment, position_bias):
    scores = scores_of(queries, key_rows, position_bias, segment)
    row_peak = jnp.max(scores, axis=-1, keepdims=True)
    exponent = jnp.exp(scores - row_peak)
    row_sum_total = jnp.sum(exponent, axis=-1, keepdims=True)
    soft_low = (exponent / row_sum_total).astype(jnp.bfloat16)
    mixture = jnp.einsum("hqk,khd->qhd", soft_low, value_rows, preferred_element_type=jnp.float32)
    return (
        mixture.reshape(queries.shape[0], -1),
        (row_peak + jnp.log(row_sum_total))[..., 0],
    )


def attend_backward(queries, key_rows, value_rows, segment, grad_rows, logsum, position_bias):
    scale = queries.shape[-1] ** (-0.5)
    scores = scores_of(queries, key_rows, position_bias, segment)
    soft = jnp.exp(scores - logsum[..., None])
    grad_soft = jnp.einsum(
        "qhd,khd->hqk", grad_rows, value_rows, preferred_element_type=jnp.float32
    )
    inner = jnp.sum(soft * grad_soft, axis=-1, keepdims=True)
    score_gradient = (soft * (grad_soft - inner)).astype(jnp.bfloat16)
    grad_query = (
        jnp.einsum("hqk,khd->qhd", score_gradient, key_rows, preferred_element_type=jnp.float32)
        * scale
    )
    grad_keys = (
        jnp.einsum("hqk,qhd->khd", score_gradient, queries, preferred_element_type=jnp.float32)
        * scale
    )
    grad_values = jnp.einsum(
        "hqk,qhd->khd", soft.astype(jnp.bfloat16), grad_rows, preferred_element_type=jnp.float32
    )
    return (grad_query, grad_keys, grad_values, diagonal_sums(score_gradient))


def gelu_pair(tensor):
    phi = 0.5 + 0.5 * lax.erf(tensor * (0.5**0.5))
    density = jnp.exp(-0.5 * tensor * tensor) * ((0.5 / math.pi) ** 0.5)
    return (tensor * phi).astype(jnp.bfloat16), (phi + tensor * density).astype(jnp.bfloat16)


def gather_weights(qkv_weight, out_weight):
    both = jnp.concatenate([qkv_weight, out_weight], axis=1)
    part = both.shape[1] // lax.axis_size("rep")
    own = lax.dynamic_slice_in_dim(both, lax.axis_index("rep") * part, part, axis=1)
    own = lax.all_gather(own, "ep", axis=0, tiled=True)
    whole = lax.all_gather(own, "rep", axis=1, tiled=True)
    return whole[:, : qkv_weight.shape[1]], whole[:, qkv_weight.shape[1] :]


def scatter_sum(partial):
    own = lax.psum_scatter(
        partial.astype(jnp.bfloat16), "rep", scatter_dimension=1, tiled=True
    )
    own = lax.psum_scatter(own, "ep", scatter_dimension=0, tiled=True)
    return lax.all_gather(own, "rep", axis=1, tiled=True)


def on_device(
    tokens,
    cotangent,
    segment_ids,
    routes,
    rel_buckets,
    qkv_weight,
    out_weight,
    router_weight,
    gains,
    bias_table,
    expert_in,
    expert_out,
):
    tok_rows = tokens.shape[0]
    width_model = tokens.shape[1]
    sequences = segment_ids.shape[0]
    sequence_length = segment_ids.shape[1]
    experts_all = router_weight.shape[1]
    local_experts = expert_in.shape[0]
    head_count = bias_table.shape[1]
    bucket_count = bias_table.shape[0]
    head_width = width_model // head_count
    groups = lax.axis_size("ep")
    capacity = max(2, 2 * tok_rows // experts_all)
    source = tokens.astype(jnp.float32)
    gain_first = gains[0]
    gain_second = gains[1]
    qkv_full, out_full = gather_weights(qkv_weight, out_weight)
    normed = rms_scale(source, gain_first).astype(jnp.bfloat16)
    packed = jnp.dot(normed, qkv_full, preferred_element_type=jnp.float32).astype(jnp.bfloat16)
    split_qkv = packed.reshape(sequences, sequence_length, 3, head_count, head_width)
    queries = split_qkv[:, :, 0]
    key_rows = split_qkv[:, :, 1]
    value_rows = split_qkv[:, :, 2]
    buckets = jnp.concatenate([rel_buckets, jnp.full((1,), -1, jnp.int32)])[::-1]
    buckets = jnp.roll(buckets, sequence_length)
    bucket_table = (
        buckets[:, None] == jnp.arange(bucket_count, dtype=jnp.int32)[None, :]
    ).astype(jnp.float32)
    bias_cols = jnp.dot(bucket_table, bias_table, precision=highest).T
    position_bias = diagonal_bias(bias_cols, sequence_length)

    def forward_one(sequence_in):
        return attend_forward(
            sequence_in[0], sequence_in[1], sequence_in[2], sequence_in[3], position_bias
        )

    mixture, logsum = lax.map(forward_one, (queries, key_rows, value_rows, segment_ids))
    mixture = mixture.reshape(tok_rows, width_model).astype(jnp.bfloat16)
    attn_out = jnp.dot(mixture, out_full, preferred_element_type=jnp.float32)
    middle = source + attn_out
    moe_in = rms_scale(middle, gain_second).astype(jnp.bfloat16)
    logits = jnp.dot(moe_in, router_weight, preferred_element_type=jnp.float32)
    router = jax.nn.softmax(logits, axis=-1)
    chosen = routes[:, 0]
    route_hot = chosen[:, None] == jnp.arange(experts_all, dtype=jnp.int32)[None, :]
    hot_float = route_hot.astype(jnp.float32)
    prob_chosen = jnp.sum(router * hot_float, axis=-1)
    chosen_gate_value = experts_all * prob_chosen
    running = jnp.cumsum(route_hot.astype(jnp.int32), axis=0)
    slot_rank = jnp.sum(jnp.where(route_hot, running, 0), axis=-1) - 1
    slot_index = chosen * capacity + slot_rank
    outgoing = (
        jnp.zeros((experts_all * capacity, width_model), jnp.bfloat16).at[slot_index].set(moe_in)
    )
    outgoing = outgoing.reshape(groups, local_experts, capacity, width_model)
    arrived = lax.all_to_all(outgoing, "ep", split_axis=0, concat_axis=0, tiled=True)
    grad_out = cotangent.astype(jnp.float32)
    grad_back = (chosen_gate_value[:, None] * grad_out).astype(jnp.bfloat16)
    incoming = (
        jnp.zeros((experts_all * capacity, width_model), jnp.bfloat16).at[slot_index].set(grad_back)
    )
    incoming = incoming.reshape(groups, local_experts, capacity, width_model)
    grad_arrived = lax.all_to_all(incoming, "ep", split_axis=0, concat_axis=0, tiled=True)
    preact = jnp.einsum("necd,edf->necf", arrived, expert_in, preferred_element_type=jnp.float32)
    activated, gelu_slope = lax.optimization_barrier(gelu_pair(preact))
    produced = jnp.einsum(
        "necf,efd->necd", activated, expert_out, preferred_element_type=jnp.float32
    ).astype(jnp.bfloat16)
    returned = lax.all_to_all(produced, "ep", split_axis=0, concat_axis=0, tiled=True)
    grad_activated = jnp.einsum(
        "necd,efd->necf", grad_arrived, expert_out, preferred_element_type=jnp.float32
    )
    grad_preact = lax.optimization_barrier((grad_activated * gelu_slope).astype(jnp.bfloat16))
    grad_dispatched = jnp.einsum(
        "necf,edf->necd", grad_preact, expert_in, preferred_element_type=jnp.float32
    ).astype(jnp.bfloat16)
    grad_sent = lax.all_to_all(grad_dispatched, "ep", split_axis=0, concat_axis=0, tiled=True)
    grad_expert_out = jnp.einsum(
        "necf,necd->efd", activated, grad_arrived, preferred_element_type=jnp.float32
    )
    grad_expert_in = jnp.einsum(
        "necd,necf->edf", arrived, grad_preact, preferred_element_type=jnp.float32
    )
    back_rows = returned.reshape(experts_all * capacity, width_model)[slot_index].astype(
        jnp.float32
    )
    output = (middle + chosen_gate_value[:, None] * back_rows).astype(jnp.bfloat16)
    grad_gate = jnp.sum(grad_out * back_rows, axis=-1)
    grad_moe_in = grad_sent.reshape(experts_all * capacity, width_model)[slot_index].astype(
        jnp.float32
    )
    grad_logits = ((experts_all * grad_gate * prob_chosen)[:, None] * (hot_float - router)).astype(
        jnp.bfloat16
    )
    grad_router = jnp.einsum("td,te->de", moe_in, grad_logits, preferred_element_type=jnp.float32)
    grad_moe_in = grad_moe_in + jnp.einsum(
        "te,de->td", grad_logits, router_weight, preferred_element_type=jnp.float32
    )
    _, second_back = jax.vjp(rms_scale, middle, gain_second)
    grad_middle_norm, grad_gain_second = second_back(grad_moe_in)
    grad_middle = grad_out + grad_middle_norm
    grad_attn = grad_middle.astype(jnp.bfloat16)
    grad_out_weight = jnp.einsum(
        "td,te->de", mixture, grad_attn, preferred_element_type=jnp.float32
    )
    grad_mixture = jnp.einsum(
        "te,de->td", grad_attn, out_full, preferred_element_type=jnp.float32
    ).astype(jnp.bfloat16)
    grad_split = grad_mixture.reshape(sequences, sequence_length, head_count, head_width)

    def backward_one(sequence_in):
        return attend_backward(
            sequence_in[0],
            sequence_in[1],
            sequence_in[2],
            sequence_in[3],
            sequence_in[4],
            sequence_in[5],
            position_bias,
        )

    grad_query, grad_keys, grad_values, bias_grads = lax.map(
        backward_one, (queries, key_rows, value_rows, segment_ids, grad_split, logsum)
    )
    grad_table = jnp.dot(bucket_table.T, jnp.sum(bias_grads, axis=0).T, precision=highest)
    grad_packed = (
        jnp.stack([grad_query, grad_keys, grad_values], axis=2)
        .reshape(tok_rows, 3 * width_model)
        .astype(jnp.bfloat16)
    )
    grad_qkv = jnp.einsum("td,te->de", normed, grad_packed, preferred_element_type=jnp.float32)
    grad_normed = jnp.einsum("te,de->td", grad_packed, qkv_full, preferred_element_type=jnp.float32)
    _, first_back = jax.vjp(rms_scale, source, gain_first)
    grad_source_norm, grad_gain_first = first_back(grad_normed)
    grad_tokens = (grad_middle + grad_source_norm).astype(jnp.bfloat16)
    router_sum, gains_sum, table_sum = lax.psum(
        (grad_router, jnp.stack([grad_gain_first, grad_gain_second]), grad_table), ("rep", "ep")
    )
    dense_qkv, dense_out = scatter_sum(grad_qkv), scatter_sum(grad_out_weight)
    expert_in_sum, expert_out_sum = (
        lax.psum(grad_expert_in.astype(jnp.bfloat16), "rep"),
        lax.psum(grad_expert_out.astype(jnp.bfloat16), "rep"),
    )
    return (
        output,
        grad_tokens,
        dense_qkv,
        dense_out,
        router_sum.astype(jnp.bfloat16),
        gains_sum.astype(jnp.bfloat16),
        table_sum.astype(jnp.bfloat16),
        expert_in_sum,
        expert_out_sum,
    )


def solution(mesh):
    return jax.shard_map(
        on_device,
        mesh=mesh,
        in_specs=(
            P(("rep", "ep"), None),
            P(("rep", "ep"), None),
            P(("rep", "ep"), None),
            P(("rep", "ep"), None),
            P(),
            P("ep", None),
            P("ep", None),
            P(),
            P(),
            P(),
            P("ep", None, None),
            P("ep", None, None),
        ),
        out_specs=(
            P(("rep", "ep"), None),
            P(("rep", "ep"), None),
            P("ep", None),
            P("ep", None),
            P(),
            P(),
            P(),
            P("ep", None, None),
            P("ep", None, None),
        ),
        check_vma=False,
    )
```

```python
import math

import jax
import jax.numpy as jnp
from jax import lax
from jax.experimental import pallas as pl
from jax.experimental.pallas import tpu as pltpu
from jax.sharding import PartitionSpec as P

epsilon = 1e-06
neg_big = -1e30
highest = lax.Precision.HIGHEST


def rms_scale(matrix, gain_row):
    return (
        matrix * lax.rsqrt(jnp.mean(matrix * matrix, axis=-1, keepdims=True) + epsilon) * gain_row
    )


def diagonal_bias_kernel(cols_ref, bias_ref):
    length = bias_ref.shape[1]
    rows = jnp.broadcast_to(cols_ref[0], (8, 2 * length))
    place = lax.broadcasted_iota(jnp.int32, rows.shape, 0)
    for step in (1, 2, 4):
        rows = jnp.where((place & step) != 0, pltpu.roll(rows, step, 1), rows)
    while rows.shape[0] < length:
        rows = jnp.concatenate([rows, pltpu.roll(rows, rows.shape[0], 1)], axis=0)
    bias_ref[0] = rows[:, :length]


def diagonal_bias(cols, length):
    heads = cols.shape[0]
    return pl.pallas_call(
        diagonal_bias_kernel,
        grid=(heads,),
        in_specs=[pl.BlockSpec((1, 1, 2 * length), lambda h: (h, 0, 0))],
        out_specs=pl.BlockSpec((1, length, length), lambda h: (h, 0, 0)),
        out_shape=jax.ShapeDtypeStruct((heads, length, length), jnp.float32),
        compiler_params=pltpu.CompilerParams(vmem_limit_bytes=32 * 1024 * 1024),
        cost_estimate=pl.CostEstimate(
            flops=heads * length * length * 4,
            bytes_accessed=heads * length * length * 4,
            transcendentals=0,
        ),
    )(cols[:, None, :])


def diagonal_sums_kernel(grad_ref, sums_ref):
    length = grad_ref.shape[1]
    rows = grad_ref[0].astype(jnp.float32)
    rows = jnp.concatenate([rows, jnp.zeros_like(rows)], axis=1)
    while rows.shape[0] > 8:
        half = rows.shape[0] // 2
        rows = rows[:half] + pltpu.roll(rows[half:], 2 * length - half, 1)
    place = lax.broadcasted_iota(jnp.int32, rows.shape, 0)
    for step in (4, 2, 1):
        rows = jnp.where((place & step) != 0, pltpu.roll(rows, 2 * length - step, 1), rows)
    sums_ref[0] = jnp.sum(rows, axis=0, keepdims=True)


def diagonal_sums(grad):
    heads, length, _ = grad.shape
    return pl.pallas_call(
        diagonal_sums_kernel,
        grid=(heads,),
        in_specs=[pl.BlockSpec((1, length, length), lambda h: (h, 0, 0))],
        out_specs=pl.BlockSpec((1, 1, 2 * length), lambda h: (h, 0, 0)),
        out_shape=jax.ShapeDtypeStruct((heads, 1, 2 * length), jnp.float32),
        compiler_params=pltpu.CompilerParams(vmem_limit_bytes=32 * 1024 * 1024),
        cost_estimate=pl.CostEstimate(
            flops=heads * length * length * 4,
            bytes_accessed=heads * length * length * 2,
            transcendentals=0,
        ),
    )(grad)[:, 0]


def scores_of(queries, key_rows, position_bias, segment):
    scores = (
        jnp.einsum("qhd,khd->hqk", queries, key_rows, preferred_element_type=jnp.float32)
        * queries.shape[-1] ** (-0.5)
        + position_bias
    )
    same_doc = segment[:, None] == segment[None, :]
    return jnp.where(same_doc[None], scores, neg_big)


def attend_forward(queries, key_rows, value_rows, segment, position_bias):
    scores = scores_of(queries, key_rows, position_bias, segment)
    row_peak = jnp.max(scores, axis=-1, keepdims=True)
    exponent = jnp.exp(scores - row_peak)
    row_sum_total = jnp.sum(exponent, axis=-1, keepdims=True)
    soft_low = (exponent / row_sum_total).astype(jnp.bfloat16)
    mixture = jnp.einsum("hqk,khd->qhd", soft_low, value_rows, preferred_element_type=jnp.float32)
    return (
        mixture.reshape(queries.shape[0], -1),
        (row_peak + jnp.log(row_sum_total))[..., 0],
    )


def attend_backward(queries, key_rows, value_rows, segment, grad_rows, logsum, position_bias):
    scale = queries.shape[-1] ** (-0.5)
    scores = scores_of(queries, key_rows, position_bias, segment)
    soft = jnp.exp(scores - logsum[..., None])
    grad_soft = jnp.einsum(
        "qhd,khd->hqk", grad_rows, value_rows, preferred_element_type=jnp.float32
    )
    inner = jnp.sum(soft * grad_soft, axis=-1, keepdims=True)
    score_gradient = (soft * (grad_soft - inner)).astype(jnp.bfloat16)
    grad_query = (
        jnp.einsum("hqk,khd->qhd", score_gradient, key_rows, preferred_element_type=jnp.float32)
        * scale
    )
    grad_keys = (
        jnp.einsum("hqk,qhd->khd", score_gradient, queries, preferred_element_type=jnp.float32)
        * scale
    )
    grad_values = jnp.einsum(
        "hqk,qhd->khd", soft.astype(jnp.bfloat16), grad_rows, preferred_element_type=jnp.float32
    )
    return (grad_query, grad_keys, grad_values, diagonal_sums(score_gradient))


def gelu_pair(tensor):
    phi = 0.5 + 0.5 * lax.erf(tensor * (0.5**0.5))
    density = jnp.exp(-0.5 * tensor * tensor) * ((0.5 / math.pi) ** 0.5)
    return (tensor * phi).astype(jnp.bfloat16), (phi + tensor * density).astype(jnp.bfloat16)


def gather_weight(weight):
    part = weight.shape[1] // lax.axis_size("rep")
    own = lax.dynamic_slice_in_dim(weight, lax.axis_index("rep") * part, part, axis=1)
    return lax.all_gather(own, "ep", axis=0, tiled=True)


def from_partner(array):
    return lax.ppermute(array, "rep", [(0, 1), (1, 0)])


def scatter_sum(partial):
    groups = lax.axis_size("ep")
    rows = partial.shape[0] // groups
    part = partial.shape[1] // 2
    core = lax.axis_index("rep")
    mine = lax.dynamic_slice_in_dim(partial, core * part, part, axis=1)
    theirs = lax.dynamic_slice_in_dim(partial, (1 - core) * part, part, axis=1)
    other = from_partner(theirs.astype(jnp.bfloat16))
    own = (mine + other.astype(jnp.float32)).astype(jnp.bfloat16)
    own = lax.all_to_all(
        own.reshape(groups, rows, part), "ep", split_axis=0, concat_axis=0, tiled=True
    )
    own = jnp.sum(own.astype(jnp.float32), axis=0).astype(jnp.bfloat16)
    return lax.all_gather(own, "rep", axis=1, tiled=True)


def pair_sum(partial):
    low = partial.astype(jnp.bfloat16)
    other = from_partner(low)
    return (low.astype(jnp.float32) + other.astype(jnp.float32)).astype(jnp.bfloat16)


def on_device(
    tokens,
    cotangent,
    segment_ids,
    routes,
    rel_buckets,
    qkv_weight,
    out_weight,
    router_weight,
    gains,
    bias_table,
    expert_in,
    expert_out,
):
    tok_rows = tokens.shape[0]
    width_model = tokens.shape[1]
    sequences = segment_ids.shape[0]
    sequence_length = segment_ids.shape[1]
    experts_all = router_weight.shape[1]
    local_experts = expert_in.shape[0]
    head_count = bias_table.shape[1]
    bucket_count = bias_table.shape[0]
    head_width = width_model // head_count
    groups = lax.axis_size("ep")
    capacity = max(2, 2 * tok_rows // experts_all)
    source = tokens.astype(jnp.float32)
    gain_first = gains[0]
    gain_second = gains[1]
    qkv_half = gather_weight(qkv_weight)
    normed = rms_scale(source, gain_first).astype(jnp.bfloat16)
    buckets = jnp.concatenate([rel_buckets, jnp.full((1,), -1, jnp.int32)])[::-1]
    buckets = jnp.roll(buckets, sequence_length)
    bucket_table = (
        buckets[:, None] == jnp.arange(bucket_count, dtype=jnp.int32)[None, :]
    ).astype(jnp.float32)
    bias_cols = jnp.dot(bucket_table, bias_table, precision=highest).T
    position_bias = diagonal_bias(bias_cols, sequence_length)
    qkv_half, out_later, normed, position_bias = lax.optimization_barrier(
        (qkv_half, out_weight, normed, position_bias)
    )
    qkv_full = lax.all_gather(qkv_half, "rep", axis=1, tiled=True)
    out_full = lax.all_gather(gather_weight(out_later), "rep", axis=1, tiled=True)
    packed = jnp.dot(normed, qkv_full, preferred_element_type=jnp.float32).astype(jnp.bfloat16)
    split_qkv = packed.reshape(sequences, sequence_length, 3, head_count, head_width)
    queries = split_qkv[:, :, 0]
    key_rows = split_qkv[:, :, 1]
    value_rows = split_qkv[:, :, 2]

    def forward_one(sequence_in):
        return attend_forward(
            sequence_in[0], sequence_in[1], sequence_in[2], sequence_in[3], position_bias
        )

    mixture, logsum = lax.map(forward_one, (queries, key_rows, value_rows, segment_ids))
    mixture = mixture.reshape(tok_rows, width_model).astype(jnp.bfloat16)
    attn_out = jnp.dot(mixture, out_full, preferred_element_type=jnp.float32)
    middle = source + attn_out
    moe_in = rms_scale(middle, gain_second).astype(jnp.bfloat16)
    logits = jnp.dot(moe_in, router_weight, preferred_element_type=jnp.float32)
    router = jax.nn.softmax(logits, axis=-1)
    chosen = routes[:, 0]
    route_hot = chosen[:, None] == jnp.arange(experts_all, dtype=jnp.int32)[None, :]
    hot_float = route_hot.astype(jnp.float32)
    prob_chosen = jnp.sum(router * hot_float, axis=-1)
    chosen_gate_value = experts_all * prob_chosen
    running = jnp.cumsum(route_hot.astype(jnp.int32), axis=0)
    slot_rank = jnp.sum(jnp.where(route_hot, running, 0), axis=-1) - 1
    slot_index = chosen * capacity + slot_rank
    outgoing = (
        jnp.zeros((experts_all * capacity, width_model), jnp.bfloat16).at[slot_index].set(moe_in)
    )
    outgoing = outgoing.reshape(groups, local_experts, capacity, width_model)
    arrived = lax.all_to_all(outgoing, "ep", split_axis=0, concat_axis=0, tiled=True)
    grad_out = cotangent.astype(jnp.float32)
    grad_back = (chosen_gate_value[:, None] * grad_out).astype(jnp.bfloat16)
    incoming = (
        jnp.zeros((experts_all * capacity, width_model), jnp.bfloat16).at[slot_index].set(grad_back)
    )
    incoming = incoming.reshape(groups, local_experts, capacity, width_model)
    grad_arrived = lax.all_to_all(incoming, "ep", split_axis=0, concat_axis=0, tiled=True)
    preact = jnp.einsum("necd,edf->necf", arrived, expert_in, preferred_element_type=jnp.float32)
    activated, gelu_slope = lax.optimization_barrier(gelu_pair(preact))
    produced = jnp.einsum(
        "necf,efd->necd", activated, expert_out, preferred_element_type=jnp.float32
    ).astype(jnp.bfloat16)
    returned = lax.all_to_all(produced, "ep", split_axis=0, concat_axis=0, tiled=True)
    grad_activated = jnp.einsum(
        "necd,efd->necf", grad_arrived, expert_out, preferred_element_type=jnp.float32
    )
    grad_preact = lax.optimization_barrier((grad_activated * gelu_slope).astype(jnp.bfloat16))
    grad_dispatched = jnp.einsum(
        "necf,edf->necd", grad_preact, expert_in, preferred_element_type=jnp.float32
    ).astype(jnp.bfloat16)
    grad_sent = lax.all_to_all(grad_dispatched, "ep", split_axis=0, concat_axis=0, tiled=True)
    grad_expert_out = jnp.einsum(
        "necf,necd->efd", activated, grad_arrived, preferred_element_type=jnp.float32
    )
    grad_expert_in = jnp.einsum(
        "necd,necf->edf", arrived, grad_preact, preferred_element_type=jnp.float32
    )
    back_rows = returned.reshape(experts_all * capacity, width_model)[slot_index].astype(
        jnp.float32
    )
    output = (middle + chosen_gate_value[:, None] * back_rows).astype(jnp.bfloat16)
    grad_gate = jnp.sum(grad_out * back_rows, axis=-1)
    grad_moe_in = grad_sent.reshape(experts_all * capacity, width_model)[slot_index].astype(
        jnp.float32
    )
    grad_logits = ((experts_all * grad_gate * prob_chosen)[:, None] * (hot_float - router)).astype(
        jnp.bfloat16
    )
    grad_router = jnp.einsum("td,te->de", moe_in, grad_logits, preferred_element_type=jnp.float32)
    grad_moe_in = grad_moe_in + jnp.einsum(
        "te,de->td", grad_logits, router_weight, preferred_element_type=jnp.float32
    )
    _, second_back = jax.vjp(rms_scale, middle, gain_second)
    grad_middle_norm, grad_gain_second = second_back(grad_moe_in)
    grad_middle = grad_out + grad_middle_norm
    grad_attn = grad_middle.astype(jnp.bfloat16)
    grad_out_weight = jnp.einsum(
        "td,te->de", mixture, grad_attn, preferred_element_type=jnp.float32
    )
    grad_mixture = jnp.einsum(
        "te,de->td", grad_attn, out_full, preferred_element_type=jnp.float32
    ).astype(jnp.bfloat16)
    grad_split = grad_mixture.reshape(sequences, sequence_length, head_count, head_width)

    def backward_one(sequence_in):
        return attend_backward(
            sequence_in[0],
            sequence_in[1],
            sequence_in[2],
            sequence_in[3],
            sequence_in[4],
            sequence_in[5],
            position_bias,
        )

    grad_query, grad_keys, grad_values, bias_grads = lax.map(
        backward_one, (queries, key_rows, value_rows, segment_ids, grad_split, logsum)
    )
    grad_table = jnp.dot(bucket_table.T, jnp.sum(bias_grads, axis=0).T, precision=highest)
    grad_packed = (
        jnp.stack([grad_query, grad_keys, grad_values], axis=2)
        .reshape(tok_rows, 3 * width_model)
        .astype(jnp.bfloat16)
    )
    grad_qkv = jnp.einsum("td,te->de", normed, grad_packed, preferred_element_type=jnp.float32)
    grad_normed = jnp.einsum("te,de->td", grad_packed, qkv_full, preferred_element_type=jnp.float32)
    _, first_back = jax.vjp(rms_scale, source, gain_first)
    grad_source_norm, grad_gain_first = first_back(grad_normed)
    grad_tokens = (grad_middle + grad_source_norm).astype(jnp.bfloat16)
    router_sum, gains_sum, table_sum = lax.psum(
        (grad_router, jnp.stack([grad_gain_first, grad_gain_second]), grad_table), ("rep", "ep")
    )
    dense_qkv, dense_out = scatter_sum(grad_qkv), scatter_sum(grad_out_weight)
    expert_in_sum, expert_out_sum = pair_sum(grad_expert_in), pair_sum(grad_expert_out)
    return (
        output,
        grad_tokens,
        dense_qkv,
        dense_out,
        router_sum.astype(jnp.bfloat16),
        gains_sum.astype(jnp.bfloat16),
        table_sum.astype(jnp.bfloat16),
        expert_in_sum,
        expert_out_sum,
    )


def solution(mesh):
    return jax.shard_map(
        on_device,
        mesh=mesh,
        in_specs=(
            P(("rep", "ep"), None),
            P(("rep", "ep"), None),
            P(("rep", "ep"), None),
            P(("rep", "ep"), None),
            P(),
            P("ep", None),
            P("ep", None),
            P(),
            P(),
            P(),
            P("ep", None, None),
            P("ep", None, None),
        ),
        out_specs=(
            P(("rep", "ep"), None),
            P(("rep", "ep"), None),
            P("ep", None),
            P("ep", None),
            P(),
            P(),
            P(),
            P("ep", None, None),
            P("ep", None, None),
        ),
        check_vma=False,
    )
```

```python
import math

import jax
import jax.numpy as jnp
from jax import lax
from jax.experimental import pallas as pl
from jax.experimental.pallas import tpu as pltpu
from jax.sharding import PartitionSpec as P

epsilon = 1e-06
neg_big = -1e30
highest = lax.Precision.HIGHEST


def rms_scale(matrix, gain_row):
    return (
        matrix * lax.rsqrt(jnp.mean(matrix * matrix, axis=-1, keepdims=True) + epsilon) * gain_row
    )


def diagonal_bias_kernel(cols_ref, bias_ref):
    length = bias_ref.shape[1]
    rows = jnp.broadcast_to(cols_ref[0], (8, 2 * length))
    place = lax.broadcasted_iota(jnp.int32, rows.shape, 0)
    for step in (1, 2, 4):
        rows = jnp.where((place & step) != 0, pltpu.roll(rows, step, 1), rows)
    while rows.shape[0] < length:
        rows = jnp.concatenate([rows, pltpu.roll(rows, rows.shape[0], 1)], axis=0)
    bias_ref[0] = rows[:, :length]


def diagonal_bias(cols, length):
    heads = cols.shape[0]
    return pl.pallas_call(
        diagonal_bias_kernel,
        grid=(heads,),
        in_specs=[pl.BlockSpec((1, 1, 2 * length), lambda h: (h, 0, 0))],
        out_specs=pl.BlockSpec((1, length, length), lambda h: (h, 0, 0)),
        out_shape=jax.ShapeDtypeStruct((heads, length, length), jnp.float32),
        compiler_params=pltpu.CompilerParams(vmem_limit_bytes=32 * 1024 * 1024),
        cost_estimate=pl.CostEstimate(
            flops=heads * length * length * 4,
            bytes_accessed=heads * length * length * 4,
            transcendentals=0,
        ),
    )(cols[:, None, :])


def diagonal_sums_kernel(grad_ref, sums_ref):
    length = grad_ref.shape[1]
    rows = grad_ref[0].astype(jnp.float32)
    rows = jnp.concatenate([rows, jnp.zeros_like(rows)], axis=1)
    while rows.shape[0] > 8:
        half = rows.shape[0] // 2
        rows = rows[:half] + pltpu.roll(rows[half:], 2 * length - half, 1)
    place = lax.broadcasted_iota(jnp.int32, rows.shape, 0)
    for step in (4, 2, 1):
        rows = jnp.where((place & step) != 0, pltpu.roll(rows, 2 * length - step, 1), rows)
    sums_ref[0] = jnp.sum(rows, axis=0, keepdims=True)


def diagonal_sums(grad):
    heads, length, _ = grad.shape
    return pl.pallas_call(
        diagonal_sums_kernel,
        grid=(heads,),
        in_specs=[pl.BlockSpec((1, length, length), lambda h: (h, 0, 0))],
        out_specs=pl.BlockSpec((1, 1, 2 * length), lambda h: (h, 0, 0)),
        out_shape=jax.ShapeDtypeStruct((heads, 1, 2 * length), jnp.float32),
        compiler_params=pltpu.CompilerParams(vmem_limit_bytes=32 * 1024 * 1024),
        cost_estimate=pl.CostEstimate(
            flops=heads * length * length * 4,
            bytes_accessed=heads * length * length * 2,
            transcendentals=0,
        ),
    )(grad)[:, 0]


def scores_of(queries, key_rows, position_bias, segment):
    scores = (
        jnp.einsum("qhd,khd->hqk", queries, key_rows, preferred_element_type=jnp.float32)
        * queries.shape[-1] ** (-0.5)
        + position_bias
    )
    same_doc = segment[:, None] == segment[None, :]
    return jnp.where(same_doc[None], scores, neg_big)


def attend_forward(queries, key_rows, value_rows, segment, position_bias):
    scores = scores_of(queries, key_rows, position_bias, segment)
    row_peak = jnp.max(scores, axis=-1, keepdims=True)
    exponent = jnp.exp(scores - row_peak)
    row_sum_total = jnp.sum(exponent, axis=-1, keepdims=True)
    soft_low = (exponent / row_sum_total).astype(jnp.bfloat16)
    mixture = jnp.einsum("hqk,khd->qhd", soft_low, value_rows, preferred_element_type=jnp.float32)
    return (
        mixture.reshape(queries.shape[0], -1),
        (row_peak + jnp.log(row_sum_total))[..., 0],
    )


def attend_backward(queries, key_rows, value_rows, segment, grad_rows, logsum, position_bias):
    scale = queries.shape[-1] ** (-0.5)
    scores = scores_of(queries, key_rows, position_bias, segment)
    soft = jnp.exp(scores - logsum[..., None])
    grad_soft = jnp.einsum(
        "qhd,khd->hqk", grad_rows, value_rows, preferred_element_type=jnp.float32
    )
    inner = jnp.sum(soft * grad_soft, axis=-1, keepdims=True)
    score_gradient = (soft * (grad_soft - inner)).astype(jnp.bfloat16)
    grad_query = (
        jnp.einsum("hqk,khd->qhd", score_gradient, key_rows, preferred_element_type=jnp.float32)
        * scale
    )
    grad_keys = (
        jnp.einsum("hqk,qhd->khd", score_gradient, queries, preferred_element_type=jnp.float32)
        * scale
    )
    grad_values = jnp.einsum(
        "hqk,qhd->khd", soft.astype(jnp.bfloat16), grad_rows, preferred_element_type=jnp.float32
    )
    return (grad_query, grad_keys, grad_values, diagonal_sums(score_gradient))


def gelu_pair(tensor):
    phi = 0.5 + 0.5 * lax.erf(tensor * (0.5**0.5))
    density = jnp.exp(-0.5 * tensor * tensor) * ((0.5 / math.pi) ** 0.5)
    return (tensor * phi).astype(jnp.bfloat16), (phi + tensor * density).astype(jnp.bfloat16)


def gather_weight(weight):
    part = weight.shape[1] // lax.axis_size("rep")
    own = lax.dynamic_slice_in_dim(weight, lax.axis_index("rep") * part, part, axis=1)
    return lax.all_gather(own, "ep", axis=0, tiled=True)


def from_partner(array):
    return lax.ppermute(array, "rep", [(0, 1), (1, 0)])


def scatter_sum(partial):
    groups = lax.axis_size("ep")
    rows = partial.shape[0] // groups
    part = partial.shape[1] // 2
    core = lax.axis_index("rep")
    mine = lax.dynamic_slice_in_dim(partial, core * part, part, axis=1)
    theirs = lax.dynamic_slice_in_dim(partial, (1 - core) * part, part, axis=1)
    other = from_partner(theirs.astype(jnp.bfloat16))
    own = (mine + other.astype(jnp.float32)).astype(jnp.bfloat16)
    own = lax.all_to_all(
        own.reshape(groups, rows, part), "ep", split_axis=0, concat_axis=0, tiled=True
    )
    own = jnp.sum(own.astype(jnp.float32), axis=0).astype(jnp.bfloat16)
    return lax.all_gather(own, "rep", axis=1, tiled=True)


def pair_sum(partial):
    low = partial.astype(jnp.bfloat16)
    other = from_partner(low)
    return (low.astype(jnp.float32) + other.astype(jnp.float32)).astype(jnp.bfloat16)


def on_device(
    tokens,
    cotangent,
    segment_ids,
    routes,
    rel_buckets,
    qkv_weight,
    out_weight,
    router_weight,
    gains,
    bias_table,
    expert_in,
    expert_out,
):
    tok_rows = tokens.shape[0]
    width_model = tokens.shape[1]
    sequences = segment_ids.shape[0]
    sequence_length = segment_ids.shape[1]
    experts_all = router_weight.shape[1]
    local_experts = expert_in.shape[0]
    head_count = bias_table.shape[1]
    bucket_count = bias_table.shape[0]
    head_width = width_model // head_count
    groups = lax.axis_size("ep")
    capacity = max(2, 2 * tok_rows // experts_all)
    source = tokens.astype(jnp.float32)
    gain_first = gains[0]
    gain_second = gains[1]
    weight_half = gather_weight(jnp.concatenate([qkv_weight, out_weight], axis=1))
    normed = rms_scale(source, gain_first).astype(jnp.bfloat16)
    buckets = jnp.concatenate([rel_buckets, jnp.full((1,), -1, jnp.int32)])[::-1]
    buckets = jnp.roll(buckets, sequence_length)
    bucket_table = (
        buckets[:, None] == jnp.arange(bucket_count, dtype=jnp.int32)[None, :]
    ).astype(jnp.float32)
    bias_cols = jnp.dot(bucket_table, bias_table, precision=highest).T
    position_bias = diagonal_bias(bias_cols, sequence_length)
    weight_half, normed, position_bias = lax.optimization_barrier(
        (weight_half, normed, position_bias)
    )
    weight_full = lax.all_gather(weight_half, "rep", axis=1, tiled=True)
    qkv_full = weight_full[:, : qkv_weight.shape[1]]
    out_full = weight_full[:, qkv_weight.shape[1] :]
    packed = jnp.dot(normed, qkv_full, preferred_element_type=jnp.float32).astype(jnp.bfloat16)
    split_qkv = packed.reshape(sequences, sequence_length, 3, head_count, head_width)
    queries = split_qkv[:, :, 0]
    key_rows = split_qkv[:, :, 1]
    value_rows = split_qkv[:, :, 2]

    def forward_one(sequence_in):
        return attend_forward(
            sequence_in[0], sequence_in[1], sequence_in[2], sequence_in[3], position_bias
        )

    mixture, logsum = lax.map(forward_one, (queries, key_rows, value_rows, segment_ids))
    mixture = mixture.reshape(tok_rows, width_model).astype(jnp.bfloat16)
    attn_out = jnp.dot(mixture, out_full, preferred_element_type=jnp.float32)
    middle = source + attn_out
    moe_in = rms_scale(middle, gain_second).astype(jnp.bfloat16)
    logits = jnp.dot(moe_in, router_weight, preferred_element_type=jnp.float32)
    router = jax.nn.softmax(logits, axis=-1)
    chosen = routes[:, 0]
    route_hot = chosen[:, None] == jnp.arange(experts_all, dtype=jnp.int32)[None, :]
    hot_float = route_hot.astype(jnp.float32)
    prob_chosen = jnp.sum(router * hot_float, axis=-1)
    chosen_gate_value = experts_all * prob_chosen
    running = jnp.cumsum(route_hot.astype(jnp.int32), axis=0)
    slot_rank = jnp.sum(jnp.where(route_hot, running, 0), axis=-1) - 1
    slot_index = chosen * capacity + slot_rank
    outgoing = (
        jnp.zeros((experts_all * capacity, width_model), jnp.bfloat16).at[slot_index].set(moe_in)
    )
    outgoing = outgoing.reshape(groups, local_experts, capacity, width_model)
    grad_out = cotangent.astype(jnp.float32)
    grad_back = (chosen_gate_value[:, None] * grad_out).astype(jnp.bfloat16)
    incoming = (
        jnp.zeros((experts_all * capacity, width_model), jnp.bfloat16).at[slot_index].set(grad_back)
    )
    incoming = incoming.reshape(groups, local_experts, capacity, width_model)
    outgoing, incoming = lax.optimization_barrier((outgoing, incoming))
    arrived = lax.all_to_all(outgoing, "ep", split_axis=0, concat_axis=0, tiled=True)
    grad_arrived = lax.all_to_all(incoming, "ep", split_axis=0, concat_axis=0, tiled=True)
    preact = jnp.einsum("necd,edf->necf", arrived, expert_in, preferred_element_type=jnp.float32)
    activated, gelu_slope = gelu_pair(preact)
    activated, gelu_slope, grad_arrived = lax.optimization_barrier(
        (activated, gelu_slope, grad_arrived)
    )
    produced = jnp.einsum(
        "necf,efd->necd", activated, expert_out, preferred_element_type=jnp.float32
    ).astype(jnp.bfloat16)
    returned = lax.all_to_all(produced, "ep", split_axis=0, concat_axis=0, tiled=True)
    grad_activated = jnp.einsum(
        "necd,efd->necf", grad_arrived, expert_out, preferred_element_type=jnp.float32
    )
    grad_preact = lax.optimization_barrier((grad_activated * gelu_slope).astype(jnp.bfloat16))
    grad_dispatched = jnp.einsum(
        "necf,edf->necd", grad_preact, expert_in, preferred_element_type=jnp.float32
    ).astype(jnp.bfloat16)
    grad_sent = lax.all_to_all(grad_dispatched, "ep", split_axis=0, concat_axis=0, tiled=True)
    grad_expert_out = jnp.einsum(
        "necf,necd->efd", activated, grad_arrived, preferred_element_type=jnp.float32
    )
    grad_expert_in = jnp.einsum(
        "necd,necf->edf", arrived, grad_preact, preferred_element_type=jnp.float32
    )
    back_rows = returned.reshape(experts_all * capacity, width_model)[slot_index].astype(
        jnp.float32
    )
    output = (middle + chosen_gate_value[:, None] * back_rows).astype(jnp.bfloat16)
    grad_gate = jnp.sum(grad_out * back_rows, axis=-1)
    grad_moe_in = grad_sent.reshape(experts_all * capacity, width_model)[slot_index].astype(
        jnp.float32
    )
    grad_logits = ((experts_all * grad_gate * prob_chosen)[:, None] * (hot_float - router)).astype(
        jnp.bfloat16
    )
    grad_router = jnp.einsum("td,te->de", moe_in, grad_logits, preferred_element_type=jnp.float32)
    grad_moe_in = grad_moe_in + jnp.einsum(
        "te,de->td", grad_logits, router_weight, preferred_element_type=jnp.float32
    )
    _, second_back = jax.vjp(rms_scale, middle, gain_second)
    grad_middle_norm, grad_gain_second = second_back(grad_moe_in)
    grad_middle = grad_out + grad_middle_norm
    grad_attn = grad_middle.astype(jnp.bfloat16)
    grad_out_weight = jnp.einsum(
        "td,te->de", mixture, grad_attn, preferred_element_type=jnp.float32
    )
    grad_mixture = jnp.einsum(
        "te,de->td", grad_attn, out_full, preferred_element_type=jnp.float32
    ).astype(jnp.bfloat16)
    grad_split = grad_mixture.reshape(sequences, sequence_length, head_count, head_width)

    def backward_one(sequence_in):
        return attend_backward(
            sequence_in[0],
            sequence_in[1],
            sequence_in[2],
            sequence_in[3],
            sequence_in[4],
            sequence_in[5],
            position_bias,
        )

    grad_query, grad_keys, grad_values, bias_grads = lax.map(
        backward_one, (queries, key_rows, value_rows, segment_ids, grad_split, logsum)
    )
    grad_table = jnp.dot(bucket_table.T, jnp.sum(bias_grads, axis=0).T, precision=highest)
    grad_packed = (
        jnp.stack([grad_query, grad_keys, grad_values], axis=2)
        .reshape(tok_rows, 3 * width_model)
        .astype(jnp.bfloat16)
    )
    grad_qkv = jnp.einsum("td,te->de", normed, grad_packed, preferred_element_type=jnp.float32)
    grad_normed = jnp.einsum("te,de->td", grad_packed, qkv_full, preferred_element_type=jnp.float32)
    _, first_back = jax.vjp(rms_scale, source, gain_first)
    grad_source_norm, grad_gain_first = first_back(grad_normed)
    grad_tokens = (grad_middle + grad_source_norm).astype(jnp.bfloat16)
    router_sum, gains_sum, table_sum = lax.psum(
        (grad_router, jnp.stack([grad_gain_first, grad_gain_second]), grad_table), ("rep", "ep")
    )
    dense_qkv, dense_out = scatter_sum(grad_qkv), scatter_sum(grad_out_weight)
    expert_in_sum, expert_out_sum = pair_sum(grad_expert_in), pair_sum(grad_expert_out)
    return (
        output,
        grad_tokens,
        dense_qkv,
        dense_out,
        router_sum.astype(jnp.bfloat16),
        gains_sum.astype(jnp.bfloat16),
        table_sum.astype(jnp.bfloat16),
        expert_in_sum,
        expert_out_sum,
    )


def solution(mesh):
    return jax.shard_map(
        on_device,
        mesh=mesh,
        in_specs=(
            P(("rep", "ep"), None),
            P(("rep", "ep"), None),
            P(("rep", "ep"), None),
            P(("rep", "ep"), None),
            P(),
            P("ep", None),
            P("ep", None),
            P(),
            P(),
            P(),
            P("ep", None, None),
            P("ep", None, None),
        ),
        out_specs=(
            P(("rep", "ep"), None),
            P(("rep", "ep"), None),
            P("ep", None),
            P("ep", None),
            P(),
            P(),
            P(),
            P("ep", None, None),
            P("ep", None, None),
        ),
        check_vma=False,
    )
```
